32 devices in a mesh: pole: 2 (over y), prow: 4 (over z), pcol: 4 (over x, core).
Axes of the slice: x: 2, y: 2, z: 4, core: 2. Of those that a mesh axis runs over, the one named last changes fastest.
Arguments:
- ginv: bfloat16 [4096, 2048], P(('pole', 'prow'), 'pcol'), parts along dimension 0, may hold values from -6 to 6
- panels: bfloat16 [8, 1024, 256], P('pole', 'prow'), parts along dimension 0, may hold values from -0.1875 to 0.1875
- structure: int32 [4, 4], replicated, may hold values from 0 to 7, all different within a row
- dinv: float32 [8, 256, 256], P('pole'), parts along dimension 0, may hold values from -6 to 6
Outputs:
- offdiag: float32 [4096, 1024], P(('pole', 'prow', 'pcol')), parts along dimension 0
- diag: float32 [8, 256, 256], P('pole'), parts along dimension 0
The draws below stay inside these ranges and needn't reach their ends.
There are 2 independent parts, one for each index of `pole`. The reference program is written for one: setup_inputs(seed, part) draws one part's arguments, and reference() takes and returns one part's arrays. A program takes and returns all parts, laid end to end along the dimension named above; an argument that names none is the same for every part. Nothing has to cross between parts.
Inputs may be any that keep to these rules, and one draw needn't show every extreme that they name: `structure`: each row names 4 different ancestor supernodes, and every ancestor supernode is named by some row.
All inputs are finite; a program needn't handle non-finite values.
Results may differ from the reference program's by a relative error of at most 0.0003.
Values may be sent and summed in bfloat16 or wider, within the bound.
A program may use at most 128 MiB of HBM per device.

```python
import jax
import jax.numpy as jnp
from jax import lax

B = 256
S = 4
NB = 8
P_SIZE = 4


def levels(own_key, shape, pieces, least, largest):
    factor_of, own = 1.0, jax.random.fold_in(own_key, 6)
    for axis_at, parts in pieces:
        heights = jnp.exp(jax.random.uniform(jax.random.fold_in(own, axis_at), (parts,), jnp.float32, least / len(pieces), largest / len(pieces)))
        factor_of = factor_of * jnp.repeat(heights, shape[axis_at] // parts).reshape([-1 if axis == axis_at else 1 for axis in range(len(shape))])
    return factor_of


def distinct(key, rows, number_of, top, lift):
    sequence = jax.random.permutation(jax.random.fold_in(key, 1), number_of)
    pull = sequence
    for power in range(3):
        pull = pull * pull // number_of
    pull = pull * lift // number_of
    tickets = jax.random.randint(jax.random.fold_in(key, 2), (rows, number_of), 0, 4096) + pull
    holders = jax.random.permutation(jax.random.fold_in(key, 3), rows)[jnp.arange(number_of) % rows]
    tickets = jnp.where(jnp.arange(rows)[:, None] == holders[None, :], 1 << 14, tickets)
    score = tickets * number_of + jnp.arange(number_of)
    return lax.top_k(score.astype(jnp.int32), top)[1].astype(jnp.int32)


def centred(rng, extent, deviation, reach, pieces=(), kind=jnp.bfloat16):
    result = jax.random.normal(rng, extent, jnp.float32) * deviation
    if len(pieces) > 0:
        result = levels(rng, extent, pieces, -0.22, 0.18) * result
    return jnp.clip(result, min=-reach, max=reach).astype(kind)


def setup_inputs(seed: int = 0, part: int = 0) -> dict:
    splits = jax.random.split(jax.random.key(seed), 5)
    part_keys = jax.random.split(jax.random.fold_in(splits[4], part), 5)
    ginv = centred(part_keys[0], (NB * B, NB * B), 1.0, 6.0, ((0, 4), (1, 4)))
    panels = centred(part_keys[1], (S, P_SIZE * B, B), (P_SIZE * B) ** -0.5, 0.1875, ((1, 4),))
    structure = distinct(splits[2], S, NB, P_SIZE, 0)
    dinv = centred(part_keys[3], (S, B, B), 1.0, 6.0, (), jnp.float32)
    return {"ginv": ginv, "panels": panels, "structure": structure, "dinv": dinv}


def reference(ginv, panels, structure, dinv):
    offsets = jnp.arange(B, dtype=jnp.int32)

    def one_super(member):
        one_panel, blocks_used = member
        columns = (blocks_used.astype(jnp.int32)[:, None] * B + offsets[None, :]).reshape(-1).astype(jnp.int32)
        chosen = jnp.take(ginv, columns, axis=1).astype(jnp.float32)
        panel_wide = one_panel.astype(jnp.float32)
        product = jnp.dot(chosen, panel_wide, precision=lax.Precision.HIGHEST)
        picked = jnp.take(product, columns, axis=0)
        diag_term = jnp.dot(jnp.transpose(panel_wide), picked, precision=lax.Precision.HIGHEST)
        return product, diag_term

    products, diag_terms = lax.map(one_super, (panels, structure))
    offdiag = -jnp.transpose(products, (1, 0, 2)).reshape(NB * B, S * B)
    return offdiag, dinv + diag_terms
```

```python
import functools

import jax
import jax.numpy as jnp
from jax import lax
from jax.experimental import pallas as pl
from jax.experimental.pallas import tpu as pltpu
from jax.sharding import PartitionSpec as P

MESH = pl.DeviceIdType.MESH
VMEM_BYTES = 48 * 1024 * 1024


def invert_kernel(
    nz, ginv_ref, panels_ref, struct_ref, dinv_ref, off_ref, diag_ref,
    g_buf, p_buf, prod, part, rs_buf, dinv_buf,
    p_send, p_recv, g_send, g_recv, o_send, o_recv,
    r_send, r_recv, a_send, a_recv, h_send, h_recv, d_sem,
):
    z = lax.axis_index("prow")
    c = lax.axis_index("pcol")
    x, k = c // 2, c % 2
    sib, nbr, dia = 2 * x + 1 - k, 2 * (1 - x) + k, 2 * (1 - x) + 1 - k
    width = panels_ref.shape[2]
    rows, cols = ginv_ref.shape
    col_blocks, row_blocks = cols // width, rows // width
    struct_count = struct_ref.shape[1]
    keep = off_ref.shape[0]
    piece = part.shape[0] // nz

    def zat(d):
        return lax.rem(z + d, nz)

    def zfrom(d):
        return lax.rem(z + nz - d, nz)

    def remote(src, dst, send, recv, zt, ct):
        return pltpu.make_async_remote_copy(
            src_ref=src, dst_ref=dst, send_sem=send, recv_sem=recv,
            device_id={"prow": zt, "pcol": ct}, device_id_type=MESH,
        )

    dinv_copy = pltpu.make_async_copy(dinv_ref.at[c, pl.ds(z * piece, piece)], dinv_buf, d_sem)
    dinv_copy.start()

    barrier = pltpu.get_barrier_semaphore()
    for d in range(1, nz):
        pl.semaphore_signal(barrier, inc=1, device_id={"prow": zat(d), "pcol": c}, device_id_type=MESH)
    for ct in (sib, nbr, dia):
        pl.semaphore_signal(barrier, inc=1, device_id={"prow": z, "pcol": ct}, device_id_type=MESH)
    pl.semaphore_wait(barrier, nz + 2)

    g_nbr, g_sib, g_fwd, panel_copies = [], [], [], []
    for h in range(col_blocks):
        src = ginv_ref.at[:, pl.ds(h * width, width)]
        dst = g_buf.at[c * col_blocks + h]
        g_nbr.append(remote(src, dst, g_send.at[0, h], g_recv.at[0, h], z, nbr))
        g_sib.append(remote(src, dst, g_send.at[1, h], g_recv.at[1, h], z, sib))
        held = g_buf.at[nbr * col_blocks + h]
        g_fwd.append(remote(held, held, g_send.at[2, h], g_recv.at[2, h], z, sib))
    for d in range(1, nz):
        panel_copies.append(
            remote(panels_ref.at[c], p_buf.at[z], p_send.at[d - 1], p_recv.at[d - 1], zat(d), c)
        )
    for copy in g_nbr + panel_copies + g_sib:
        copy.start()
    p_buf[z] = panels_ref[c]
    for h in range(col_blocks):
        g_buf[c * col_blocks + h] = ginv_ref[:, h * width:(h + 1) * width]
    for h in range(col_blocks):
        g_nbr[h].wait_recv()
        g_fwd[h].start()
    for copy in panel_copies + g_sib + g_fwd:
        copy.wait_recv()

    for at in range(0, rows, keep):
        acc = jnp.zeros((keep, width), jnp.float32)
        for p in range(struct_count):
            acc += jnp.dot(
                g_buf[struct_ref[c, p], pl.ds(at, keep), :], p_buf[p],
                preferred_element_type=jnp.float32,
            )
        prod[at:at + keep, :] = acc

    own_cols = pl.ds(pl.multiple_of(c * width, width), width)
    off_copies = []
    for at, ct in enumerate((nbr, dia, sib)):
        off_copies.append(
            remote(prod.at[pl.ds(ct * keep, keep)], off_ref.at[:, own_cols], o_send.at[at], o_recv.at[at], z, ct)
        )

    total = jnp.zeros((width, width), jnp.float32)
    for b in range(row_blocks):
        target = z * row_blocks + b
        place, named = jnp.int32(0), jnp.int32(0)
        for p in range(struct_count):
            hit = struct_ref[c, p] == target
            place = jnp.where(hit, p, place)
            named = jnp.where(hit, 1, named)
        right = prod[b * width:(b + 1) * width, :]
        high = right.astype(jnp.bfloat16)
        low = (right - high.astype(jnp.float32)).astype(jnp.bfloat16)
        left = p_buf[place]
        contract = (((0,), (0,)), ((), ()))
        term = lax.dot_general(left, high, contract, preferred_element_type=jnp.float32)
        term += lax.dot_general(left, low, contract, preferred_element_type=jnp.float32)
        total += term * named.astype(jnp.float32)
    part[...] = total

    sum_copies = []
    for d in range(1, nz):
        sum_copies.append(
            remote(part.at[pl.ds(zat(d) * piece, piece)], rs_buf.at[d - 1], r_send.at[d - 1], r_recv.at[d - 1], zat(d), c)
        )
    for copy in sum_copies + off_copies:
        copy.start()
    off_ref[:, own_cols] = prod[pl.ds(c * keep, keep), :]

    dinv_copy.wait()
    final = dinv_buf[...] + part[pl.ds(z * piece, piece), :]
    for d in range(1, nz):
        sum_copies[d - 1].wait_recv()
        final += rs_buf[d - 1]
    diag_ref[c, pl.ds(z * piece, piece), :] = final

    over_z, over_x, over_k, over_f = [], [], [], []
    for d in range(nz):
        mine = diag_ref.at[c, pl.ds(zfrom(d) * piece, piece)]
        theirs = diag_ref.at[nbr, pl.ds(zfrom(d) * piece, piece)]
        if d > 0:
            own = diag_ref.at[c, pl.ds(z * piece, piece)]
            over_z.append(remote(own, own, a_send.at[d - 1], a_recv.at[d - 1], zat(d), c))
        over_x.append(remote(mine, mine, h_send.at[0, d], h_recv.at[0, d], z, nbr))
        over_k.append(remote(mine, mine, h_send.at[1, d], h_recv.at[1, d], z, sib))
        over_f.append(remote(theirs, theirs, h_send.at[2, d], h_recv.at[2, d], z, sib))
    for copy in over_z:
        copy.start()
    for d in range(nz):
        if d > 0:
            over_z[d - 1].wait_recv()
        over_x[d].start()
        over_k[d].start()
    for d in range(nz):
        over_x[d].wait_recv()
        over_f[d].start()
    for copy in off_copies + over_k + over_f:
        copy.wait_recv()
    for copy in g_nbr + g_sib + g_fwd + panel_copies + off_copies + sum_copies + over_z + over_x + over_k + over_f:
        copy.wait_send()


def per_device(ginv, panels, structure, dinv):
    super_count, _, width = panels.shape
    nz, nc = lax.axis_size("prow"), lax.axis_size("pcol")
    rows, cols = ginv.shape
    struct_count = structure.shape[1]
    col_blocks = cols // width
    piece = width // nz
    vmem = pl.BlockSpec(memory_space=pltpu.VMEM)
    dma = pltpu.SemaphoreType.DMA
    off, diag = pl.pallas_call(
        functools.partial(invert_kernel, nz),
        out_shape=(
            jax.ShapeDtypeStruct((rows // nc, super_count * width), jnp.float32),
            jax.ShapeDtypeStruct((super_count, width, width), jnp.float32),
        ),
        in_specs=[vmem, vmem, pl.BlockSpec(memory_space=pltpu.SMEM), pl.BlockSpec(memory_space=pl.ANY)],
        out_specs=(vmem, vmem),
        scratch_shapes=[
            pltpu.VMEM((nc * col_blocks, rows, width), jnp.bfloat16),
            pltpu.VMEM((struct_count, width, width), jnp.bfloat16),
            pltpu.VMEM((rows, width), jnp.float32),
            pltpu.VMEM((width, width), jnp.float32),
            pltpu.VMEM((nz - 1, piece, width), jnp.float32),
            pltpu.VMEM((piece, width), jnp.float32),
            dma((nz - 1,)), dma((nz - 1,)),
            dma((3, col_blocks)), dma((3, col_blocks)),
            dma((3,)), dma((3,)),
            dma((nz - 1,)), dma((nz - 1,)),
            dma((nz - 1,)), dma((nz - 1,)),
            dma((3, nz)), dma((3, nz)),
            dma,
        ],
        compiler_params=pltpu.CompilerParams(
            collective_id=0, has_side_effects=True, vmem_limit_bytes=VMEM_BYTES
        ),
        name="selected_inverse",
    )(ginv, panels, structure, dinv)
    return -off, diag


def solution(mesh):
    return jax.shard_map(
        per_device,
        mesh=mesh,
        in_specs=(P(("pole", "prow"), "pcol"), P("pole", "prow", None), P(), P("pole", None, None)),
        out_specs=(P(("pole", "prow", "pcol"), None), P("pole", None, None)),
        check_vma=False,
    )
```

```python
import functools

import jax
import jax.numpy as jnp
from jax import lax
from jax.experimental import pallas as pl
from jax.experimental.pallas import tpu as pltpu
from jax.sharding import PartitionSpec as P

MESH = pl.DeviceIdType.MESH
VMEM_BYTES = 60 * 1024 * 1024


def invert_kernel(
    nz, ginv_ref, panels_ref, struct_hbm, dinv_ref, off_hbm, diag_hbm,
    struct_ref, g_buf, p_buf, prod, neg, part, rs_buf, dinv_buf, off_ref, diag_ref,
    p_send, p_recv, g_send, g_recv, o_send, o_recv,
    r_send, r_recv, a_send, a_recv, h_send, h_recv, l_sem,
):
    z = lax.axis_index("prow")
    c = lax.axis_index("pcol")
    x, k = c // 2, c % 2
    sib, nbr, dia = 2 * x + 1 - k, 2 * (1 - x) + k, 2 * (1 - x) + 1 - k
    width = panels_ref.shape[2]
    rows, cols = ginv_ref.shape
    col_blocks, row_blocks = cols // width, rows // width
    struct_count = struct_ref.shape[1]
    keep = off_ref.shape[0]
    piece = part.shape[0] // nz

    def zat(d):
        return lax.rem(z + d, nz)

    def zfrom(d):
        return lax.rem(z + nz - d, nz)

    def remote(src, dst, send, recv, zt, ct):
        return pltpu.make_async_remote_copy(
            src_ref=src, dst_ref=dst, send_sem=send, recv_sem=recv,
            device_id={"prow": zt, "pcol": ct}, device_id_type=MESH,
        )

    dinv_copy = pltpu.make_async_copy(dinv_ref.at[c, pl.ds(z * piece, piece)], dinv_buf, l_sem.at[0])
    struct_copy = pltpu.make_async_copy(struct_hbm, struct_ref, l_sem.at[1])
    own_copies = [pltpu.make_async_copy(panels_ref.at[c], p_buf.at[z], l_sem.at[2])]
    for h in range(col_blocks):
        src = ginv_ref.at[:, pl.ds(h * width, width)]
        own_copies.append(pltpu.make_async_copy(src, g_buf.at[c * col_blocks + h], l_sem.at[3 + h]))
    for copy in [struct_copy, dinv_copy] + own_copies:
        copy.start()

    barrier = pltpu.get_barrier_semaphore()
    for d in range(1, nz):
        pl.semaphore_signal(barrier, inc=1, device_id={"prow": zat(d), "pcol": c}, device_id_type=MESH)
    for ct in (sib, nbr, dia):
        pl.semaphore_signal(barrier, inc=1, device_id={"prow": z, "pcol": ct}, device_id_type=MESH)
    pl.semaphore_wait(barrier, nz + 2)

    g_nbr, g_sib, g_fwd, panel_copies = [], [], [], []
    for h in range(col_blocks):
        src = ginv_ref.at[:, pl.ds(h * width, width)]
        dst = g_buf.at[c * col_blocks + h]
        g_nbr.append(remote(src, dst, g_send.at[0, h], g_recv.at[0, h], z, nbr))
        g_sib.append(remote(src, dst, g_send.at[1, h], g_recv.at[1, h], z, sib))
        held = g_buf.at[nbr * col_blocks + h]
        g_fwd.append(remote(held, held, g_send.at[2, h], g_recv.at[2, h], z, sib))
    for d in range(1, nz):
        panel_copies.append(
            remote(panels_ref.at[c], p_buf.at[z], p_send.at[d - 1], p_recv.at[d - 1], zat(d), c)
        )
    for copy in g_nbr + panel_copies + g_sib:
        copy.start()
    for h in range(col_blocks):
        g_nbr[h].wait_recv()
        g_fwd[h].start()
    for copy in panel_copies + g_sib + g_fwd:
        copy.wait_recv()
    for copy in own_copies + [struct_copy]:
        copy.wait()

    for at in range(0, rows, keep):
        acc = jnp.zeros((keep, width), jnp.float32)
        for p in range(struct_count):
            acc += jnp.dot(
                g_buf[struct_ref[c, p], pl.ds(at, keep), :], p_buf[p],
                preferred_element_type=jnp.float32,
            )
        prod[at:at + keep, :] = acc
        neg[at:at + keep, :] = -acc

    own_cols = pl.ds(pl.multiple_of(c * width, width), width)
    off_copies = []
    for at, ct in enumerate((nbr, dia, sib)):
        off_copies.append(
            remote(neg.at[pl.ds(ct * keep, keep)], off_ref.at[:, own_cols], o_send.at[at], o_recv.at[at], z, ct)
        )

    total = jnp.zeros((width, width), jnp.float32)
    for b in range(row_blocks):
        target = z * row_blocks + b
        place, named = jnp.int32(0), jnp.int32(0)
        for p in range(struct_count):
            hit = struct_ref[c, p] == target
            place = jnp.where(hit, p, place)
            named = jnp.where(hit, 1, named)
        right = prod[b * width:(b + 1) * width, :]
        high = right.astype(jnp.bfloat16)
        low = (right - high.astype(jnp.float32)).astype(jnp.bfloat16)
        left = p_buf[place]
        contract = (((0,), (0,)), ((), ()))
        term = lax.dot_general(left, high, contract, preferred_element_type=jnp.float32)
        term += lax.dot_general(left, low, contract, preferred_element_type=jnp.float32)
        total += term * named.astype(jnp.float32)
    part[...] = total

    sum_copies = []
    for d in range(1, nz):
        sum_copies.append(
            remote(part.at[pl.ds(zat(d) * piece, piece)], rs_buf.at[d - 1], r_send.at[d - 1], r_recv.at[d - 1], zat(d), c)
        )
    for copy in sum_copies + off_copies:
        copy.start()
    off_ref[:, own_cols] = neg[pl.ds(c * keep, keep), :]

    dinv_copy.wait()
    final = dinv_buf[...] + part[pl.ds(z * piece, piece), :]
    for d in range(1, nz):
        sum_copies[d - 1].wait_recv()
        final += rs_buf[d - 1]
    diag_ref[c, pl.ds(z * piece, piece), :] = final

    over_z, over_x, over_k, over_f = [], [], [], []
    for d in range(nz):
        mine = diag_ref.at[c, pl.ds(zfrom(d) * piece, piece)]
        theirs = diag_ref.at[nbr, pl.ds(zfrom(d) * piece, piece)]
        if d > 0:
            own = diag_ref.at[c, pl.ds(z * piece, piece)]
            over_z.append(remote(own, own, a_send.at[d - 1], a_recv.at[d - 1], zat(d), c))
        over_x.append(remote(mine, mine, h_send.at[0, d], h_recv.at[0, d], z, nbr))
        over_k.append(remote(mine, mine, h_send.at[1, d], h_recv.at[1, d], z, sib))
        over_f.append(remote(theirs, theirs, h_send.at[2, d], h_recv.at[2, d], z, sib))
    for copy in over_z:
        copy.start()
    for d in range(nz):
        if d > 0:
            over_z[d - 1].wait_recv()
        over_x[d].start()
        over_k[d].start()
    for d in range(nz):
        over_x[d].wait_recv()
        over_f[d].start()
    for copy in off_copies:
        copy.wait_recv()
    off_out = pltpu.make_async_copy(off_ref, off_hbm, l_sem.at[3 + col_blocks])
    off_out.start()
    for copy in over_k + over_f:
        copy.wait_recv()
    diag_out = pltpu.make_async_copy(diag_ref, diag_hbm, l_sem.at[4 + col_blocks])
    diag_out.start()
    for copy in g_nbr + g_sib + g_fwd + panel_copies + off_copies + sum_copies + over_z + over_x + over_k + over_f:
        copy.wait_send()
    off_out.wait()
    diag_out.wait()


def place_kernel(off_ref, diag_ref, off_out, diag_out, off_buf, diag_buf, sem):
    step = off_ref.shape[0] // 2
    parts = [(off_ref, off_out, off_buf, pl.ds(at * step, step)) for at in range(2)]
    parts += [(diag_ref, diag_out, diag_buf, at) for at in range(diag_ref.shape[0])]
    loads, stores = [], []
    for n, (src, dst, buf, part) in enumerate(parts):
        loads.append(pltpu.make_async_copy(src.at[part], buf.at[part], sem.at[0, n]))
        stores.append(pltpu.make_async_copy(buf.at[part], dst.at[part], sem.at[1, n]))
    for copy in loads:
        copy.start()
    for load, store in zip(loads, stores):
        load.wait()
        store.start()
    for copy in stores:
        copy.wait()


def per_device(ginv, panels, structure, dinv):
    super_count, _, width = panels.shape
    nz, nc = lax.axis_size("prow"), lax.axis_size("pcol")
    rows, cols = ginv.shape
    struct_count = structure.shape[1]
    col_blocks = cols // width
    piece = width // nz
    hbm = pl.BlockSpec(memory_space=pl.ANY)
    dma = pltpu.SemaphoreType.DMA
    out_shape = (
        jax.ShapeDtypeStruct((rows // nc, super_count * width), jnp.float32),
        jax.ShapeDtypeStruct((super_count, width, width), jnp.float32),
    )
    off, diag = pl.pallas_call(
        functools.partial(invert_kernel, nz),
        out_shape=out_shape,
        in_specs=[hbm, hbm, hbm, hbm],
        out_specs=(hbm, hbm),
        scratch_shapes=[
            pltpu.SMEM((super_count, struct_count), jnp.int32),
            pltpu.VMEM((nc * col_blocks, rows, width), jnp.bfloat16),
            pltpu.VMEM((struct_count, width, width), jnp.bfloat16),
            pltpu.VMEM((rows, width), jnp.float32),
            pltpu.VMEM((rows, width), jnp.float32),
            pltpu.VMEM((width, width), jnp.float32),
            pltpu.VMEM((nz - 1, piece, width), jnp.float32),
            pltpu.VMEM((piece, width), jnp.float32),
            pltpu.VMEM((rows // nc, super_count * width), jnp.float32),
            pltpu.VMEM((super_count, width, width), jnp.float32),
            dma((nz - 1,)), dma((nz - 1,)),
            dma((3, col_blocks)), dma((3, col_blocks)),
            dma((3,)), dma((3,)),
            dma((nz - 1,)), dma((nz - 1,)),
            dma((nz - 1,)), dma((nz - 1,)),
            dma((3, nz)), dma((3, nz)),
            dma((5 + col_blocks,)),
        ],
        compiler_params=pltpu.CompilerParams(
            collective_id=0, has_side_effects=True, vmem_limit_bytes=VMEM_BYTES
        ),
        name="selected_inverse",
    )(ginv, panels, structure, dinv)
    return pl.pallas_call(
        place_kernel,
        out_shape=out_shape,
        in_specs=[hbm, hbm],
        out_specs=(hbm, hbm),
        scratch_shapes=[
            pltpu.VMEM((rows // nc, super_count * width), jnp.float32),
            pltpu.VMEM((super_count, width, width), jnp.float32),
            dma((2, 2 + super_count)),
        ],
        compiler_params=pltpu.CompilerParams(vmem_limit_bytes=VMEM_BYTES),
        name="place_outputs",
    )(off, diag)


def solution(mesh):
    return jax.shard_map(
        per_device,
        mesh=mesh,
        in_specs=(P(("pole", "prow"), "pcol"), P("pole", "prow", None), P(), P("pole", None, None)),
        out_specs=(P(("pole", "prow", "pcol"), None), P("pole", None, None)),
        check_vma=False,
    )
```

```python
import functools

import jax
import jax.numpy as jnp
from jax import lax
from jax.experimental import pallas as pl
from jax.experimental.pallas import tpu as pltpu
from jax.sharding import PartitionSpec as P

MESH = pl.DeviceIdType.MESH
VMEM_BYTES = 60 * 1024 * 1024
TILE = 16
LEVELS = 32000.0


def invert_kernel(
    nz, ginv_ref, panels_ref, struct_hbm, dinv_ref, off_hbm, diag_hbm,
    struct_ref, g_buf, p_buf, prod, neg, part, rs_buf, dinv_buf, off_ref, diag_ref, code,
    p_send, p_recv, g_send, g_recv, o_send, o_recv,
    r_send, r_recv, a_send, a_recv, h_send, h_recv, l_sem,
):
    z = lax.axis_index("prow")
    c = lax.axis_index("pcol")
    x, k = c // 2, c % 2
    sib, nbr, dia = 2 * x + 1 - k, 2 * (1 - x) + k, 2 * (1 - x) + 1 - k
    width = panels_ref.shape[2]
    rows, cols = ginv_ref.shape
    col_blocks, row_blocks = cols // width, rows // width
    struct_count = struct_ref.shape[1]
    keep = off_ref.shape[0]
    piece = part.shape[0] // nz

    def zat(d):
        return lax.rem(z + d, nz)

    def zfrom(d):
        return lax.rem(z + nz - d, nz)

    def remote(src, dst, send, recv, zt, ct):
        return pltpu.make_async_remote_copy(
            src_ref=src, dst_ref=dst, send_sem=send, recv_sem=recv,
            device_id={"prow": zt, "pcol": ct}, device_id_type=MESH,
        )

    dinv_copy = pltpu.make_async_copy(dinv_ref.at[c, pl.ds(z * piece, piece)], dinv_buf, l_sem.at[0])
    struct_copy = pltpu.make_async_copy(struct_hbm, struct_ref, l_sem.at[1])
    own_copies = [pltpu.make_async_copy(panels_ref.at[c], p_buf.at[z], l_sem.at[2])]
    for h in range(col_blocks):
        src = ginv_ref.at[:, pl.ds(h * width, width)]
        own_copies.append(pltpu.make_async_copy(src, g_buf.at[c * col_blocks + h], l_sem.at[3 + h]))
    for copy in [struct_copy, dinv_copy] + own_copies:
        copy.start()

    barrier = pltpu.get_barrier_semaphore()
    for d in range(1, nz):
        pl.semaphore_signal(barrier, inc=1, device_id={"prow": zat(d), "pcol": c}, device_id_type=MESH)
    for ct in (sib, nbr, dia):
        pl.semaphore_signal(barrier, inc=1, device_id={"prow": z, "pcol": ct}, device_id_type=MESH)
    pl.semaphore_wait(barrier, nz + 2)

    g_nbr, g_sib, g_fwd, panel_copies = [], [], [], []
    for h in range(col_blocks):
        src = ginv_ref.at[:, pl.ds(h * width, width)]
        dst = g_buf.at[c * col_blocks + h]
        g_nbr.append(remote(src, dst, g_send.at[0, h], g_recv.at[0, h], z, nbr))
        g_sib.append(remote(src, dst, g_send.at[1, h], g_recv.at[1, h], z, sib))
        held = g_buf.at[nbr * col_blocks + h]
        g_fwd.append(remote(held, held, g_send.at[2, h], g_recv.at[2, h], z, sib))
    for d in range(1, nz):
        panel_copies.append(
            remote(panels_ref.at[c], p_buf.at[z], p_send.at[d - 1], p_recv.at[d - 1], zat(d), c)
        )
    for copy in g_nbr + panel_copies + g_sib:
        copy.start()
    for h in range(col_blocks):
        g_nbr[h].wait_recv()
        g_fwd[h].start()
    for copy in panel_copies + g_sib + g_fwd:
        copy.wait_recv()
    for copy in own_copies + [struct_copy]:
        copy.wait()

    for at in range(0, rows, keep):
        acc = jnp.zeros((keep, width), jnp.float32)
        for p in range(struct_count):
            acc += jnp.dot(
                g_buf[struct_ref[c, p], pl.ds(at, keep), :], p_buf[p],
                preferred_element_type=jnp.float32,
            )
        prod[at:at + keep, :] = acc
        neg[at:at + keep, :] = -acc

    own_cols = pl.ds(pl.multiple_of(c * width, width), width)
    off_copies = []
    for at, ct in enumerate((nbr, dia, sib)):
        off_copies.append(
            remote(neg.at[pl.ds(ct * keep, keep)], off_ref.at[:, own_cols], o_send.at[at], o_recv.at[at], z, ct)
        )

    total = jnp.zeros((width, width), jnp.float32)
    for b in range(row_blocks):
        target = z * row_blocks + b
        place, named = jnp.int32(0), jnp.int32(0)
        for p in range(struct_count):
            hit = struct_ref[c, p] == target
            place = jnp.where(hit, p, place)
            named = jnp.where(hit, 1, named)
        right = prod[b * width:(b + 1) * width, :]
        high = right.astype(jnp.bfloat16)
        low = (right - high.astype(jnp.float32)).astype(jnp.bfloat16)
        left = p_buf[place]
        contract = (((0,), (0,)), ((), ()))
        term = lax.dot_general(left, high, contract, preferred_element_type=jnp.float32)
        term += lax.dot_general(left, low, contract, preferred_element_type=jnp.float32)
        total += term * named.astype(jnp.float32)
    part[...] = total

    sum_copies = []
    for d in range(1, nz):
        sum_copies.append(
            remote(part.at[pl.ds(zat(d) * piece, piece)], rs_buf.at[d - 1], r_send.at[d - 1], r_recv.at[d - 1], zat(d), c)
        )
    for copy in sum_copies + off_copies:
        copy.start()
    off_ref[:, own_cols] = neg[pl.ds(c * keep, keep), :]

    dinv_copy.wait()
    final = dinv_buf[...] + part[pl.ds(z * piece, piece), :]
    for d in range(1, nz):
        sum_copies[d - 1].wait_recv()
        final += rs_buf[d - 1]
    coded = piece % TILE == 0

    def at_piece(ct, j):
        return code.at[ct, j] if coded else diag_ref.at[ct, pl.ds(j * piece, piece)]

    def decode(ct, j):
        if coded:
            power = code[ct, j, piece:, :].astype(jnp.float32)[:1, :]
            step = jnp.exp2(power) * (1.0 / LEVELS)
            diag_ref[ct, pl.ds(j * piece, piece), :] = code[ct, j, :piece, :].astype(jnp.float32) * step

    if coded:
        largest = jnp.max(jnp.abs(final), axis=0, keepdims=True)
        power = jnp.ceil(jnp.log2(jnp.maximum(largest, 1e-30)))
        whole = jnp.round(final * (jnp.exp2(-power) * LEVELS)).astype(jnp.int32)
        code[c, z, :piece, :] = whole.astype(jnp.int16)
        below = jnp.broadcast_to(power, (TILE, width)).astype(jnp.int32)
        code[c, z, piece:, :] = below.astype(jnp.int16)
    else:
        diag_ref[c, pl.ds(z * piece, piece), :] = final

    over_z, over_x, over_k, over_f = [], [], [], []
    for d in range(nz):
        mine, theirs = at_piece(c, zfrom(d)), at_piece(nbr, zfrom(d))
        if d > 0:
            own = at_piece(c, z)
            over_z.append(remote(own, own, a_send.at[d - 1], a_recv.at[d - 1], zat(d), c))
        over_x.append(remote(mine, mine, h_send.at[0, d], h_recv.at[0, d], z, nbr))
        over_k.append(remote(mine, mine, h_send.at[1, d], h_recv.at[1, d], z, sib))
        over_f.append(remote(theirs, theirs, h_send.at[2, d], h_recv.at[2, d], z, sib))
    for copy in over_z:
        copy.start()
    for d in range(nz):
        if d > 0:
            over_z[d - 1].wait_recv()
        over_x[d].start()
        over_k[d].start()
        decode(c, zfrom(d))
    for d in range(nz):
        over_x[d].wait_recv()
        over_f[d].start()
        decode(nbr, zfrom(d))
    for copy in off_copies:
        copy.wait_recv()
    off_out = pltpu.make_async_copy(off_ref, off_hbm, l_sem.at[3 + col_blocks])
    off_out.start()
    for copies, ct in ((over_k, sib), (over_f, dia)):
        for d in range(nz):
            copies[d].wait_recv()
            decode(ct, zfrom(d))
    diag_out = pltpu.make_async_copy(diag_ref, diag_hbm, l_sem.at[4 + col_blocks])
    diag_out.start()
    for copy in g_nbr + g_sib + g_fwd + panel_copies + off_copies + sum_copies + over_z + over_x + over_k + over_f:
        copy.wait_send()
    off_out.wait()
    diag_out.wait()


def place_kernel(off_ref, diag_ref, off_out, diag_out, off_buf, diag_buf, sem):
    step = off_ref.shape[0] // 2
    parts = [(off_ref, off_out, off_buf, pl.ds(at * step, step)) for at in range(2)]
    parts += [(diag_ref, diag_out, diag_buf, at) for at in range(diag_ref.shape[0])]
    loads, stores = [], []
    for n, (src, dst, buf, part) in enumerate(parts):
        loads.append(pltpu.make_async_copy(src.at[part], buf.at[part], sem.at[0, n]))
        stores.append(pltpu.make_async_copy(buf.at[part], dst.at[part], sem.at[1, n]))
    for copy in loads:
        copy.start()
    for load, store in zip(loads, stores):
        load.wait()
        store.start()
    for copy in stores:
        copy.wait()


def per_device(ginv, panels, structure, dinv):
    super_count, _, width = panels.shape
    nz, nc = lax.axis_size("prow"), lax.axis_size("pcol")
    rows, cols = ginv.shape
    struct_count = structure.shape[1]
    col_blocks = cols // width
    piece = width // nz
    hbm = pl.BlockSpec(memory_space=pl.ANY)
    dma = pltpu.SemaphoreType.DMA
    out_shape = (
        jax.ShapeDtypeStruct((rows // nc, super_count * width), jnp.float32),
        jax.ShapeDtypeStruct((super_count, width, width), jnp.float32),
    )
    off, diag = pl.pallas_call(
        functools.partial(invert_kernel, nz),
        out_shape=out_shape,
        in_specs=[hbm, hbm, hbm, hbm],
        out_specs=(hbm, hbm),
        scratch_shapes=[
            pltpu.SMEM((super_count, struct_count), jnp.int32),
            pltpu.VMEM((nc * col_blocks, rows, width), jnp.bfloat16),
            pltpu.VMEM((struct_count, width, width), jnp.bfloat16),
            pltpu.VMEM((rows, width), jnp.float32),
            pltpu.VMEM((rows, width), jnp.float32),
            pltpu.VMEM((width, width), jnp.float32),
            pltpu.VMEM((nz - 1, piece, width), jnp.float32),
            pltpu.VMEM((piece, width), jnp.float32),
            pltpu.VMEM((rows // nc, super_count * width), jnp.float32),
            pltpu.VMEM((super_count, width, width), jnp.float32),
            pltpu.VMEM((super_count, nz, piece + TILE, width), jnp.int16)
            if piece % TILE == 0 else pltpu.VMEM((8, 128), jnp.float32),
            dma((nz - 1,)), dma((nz - 1,)),
            dma((3, col_blocks)), dma((3, col_blocks)),
            dma((3,)), dma((3,)),
            dma((nz - 1,)), dma((nz - 1,)),
            dma((nz - 1,)), dma((nz - 1,)),
            dma((3, nz)), dma((3, nz)),
            dma((5 + col_blocks,)),
        ],
        compiler_params=pltpu.CompilerParams(
            collective_id=0, has_side_effects=True, vmem_limit_bytes=VMEM_BYTES
        ),
        name="selected_inverse",
    )(ginv, panels, structure, dinv)
    return pl.pallas_call(
        place_kernel,
        out_shape=out_shape,
        in_specs=[hbm, hbm],
        out_specs=(hbm, hbm),
        scratch_shapes=[
            pltpu.VMEM((rows // nc, super_count * width), jnp.float32),
            pltpu.VMEM((super_count, width, width), jnp.float32),
            dma((2, 2 + super_count)),
        ],
        compiler_params=pltpu.CompilerParams(vmem_limit_bytes=VMEM_BYTES),
        name="place_outputs",
    )(off, diag)


def solution(mesh):
    return jax.shard_map(
        per_device,
        mesh=mesh,
        in_specs=(P(("pole", "prow"), "pcol"), P("pole", "prow", None), P(), P("pole", None, None)),
        out_specs=(P(("pole", "prow", "pcol"), None), P("pole", None, None)),
        check_vma=False,
    )
```

```python
import functools

import jax
import jax.numpy as jnp
from jax import lax
from jax.experimental import pallas as pl
from jax.experimental.pallas import tpu as pltpu
from jax.sharding import PartitionSpec as P

MESH = pl.DeviceIdType.MESH
VMEM_BYTES = 60 * 1024 * 1024
TILE = 16
LEVELS = 32000.0


def invert_kernel(
    nz, ginv_ref, panels_ref, struct_hbm, dinv_ref, off_hbm, diag_hbm,
    struct_ref, g_buf, p_buf, prod, neg, part, rs_buf, dinv_buf, off_ref, diag_ref, code,
    p_send, p_recv, g_send, g_recv, o_send, o_recv,
    r_send, r_recv, a_send, a_recv, h_send, h_recv, l_sem,
):
    z = lax.axis_index("prow")
    c = lax.axis_index("pcol")
    x, k = c // 2, c % 2
    sib, nbr, dia = 2 * x + 1 - k, 2 * (1 - x) + k, 2 * (1 - x) + 1 - k
    width = panels_ref.shape[2]
    rows, cols = ginv_ref.shape
    col_blocks, row_blocks = cols // width, rows // width
    struct_count = struct_ref.shape[1]
    keep = off_ref.shape[0]
    piece = part.shape[0] // nz

    def zat(d):
        return lax.rem(z + d, nz)

    def zfrom(d):
        return lax.rem(z + nz - d, nz)

    def remote(src, dst, send, recv, zt, ct):
        return pltpu.make_async_remote_copy(
            src_ref=src, dst_ref=dst, send_sem=send, recv_sem=recv,
            device_id={"prow": zt, "pcol": ct}, device_id_type=MESH,
        )

    dinv_copy = pltpu.make_async_copy(dinv_ref.at[c, pl.ds(z * piece, piece)], dinv_buf, l_sem.at[0])
    struct_copy = pltpu.make_async_copy(struct_hbm, struct_ref, l_sem.at[1])
    own_copies = [pltpu.make_async_copy(panels_ref.at[c], p_buf.at[z], l_sem.at[2])]
    for h in range(col_blocks):
        src = ginv_ref.at[:, pl.ds(h * width, width)]
        own_copies.append(pltpu.make_async_copy(src, g_buf.at[c * col_blocks + h], l_sem.at[3 + h]))
    for copy in [struct_copy, dinv_copy] + own_copies:
        copy.start()

    barrier = pltpu.get_barrier_semaphore()
    for d in range(1, nz):
        pl.semaphore_signal(barrier, inc=1, device_id={"prow": zat(d), "pcol": c}, device_id_type=MESH)
    for ct in (sib, nbr, dia):
        pl.semaphore_signal(barrier, inc=1, device_id={"prow": z, "pcol": ct}, device_id_type=MESH)
    pl.semaphore_wait(barrier, nz + 2)

    g_nbr, g_sib, g_fwd, panel_copies = [], [], [], []
    for h in range(col_blocks):
        src = ginv_ref.at[:, pl.ds(h * width, width)]
        dst = g_buf.at[c * col_blocks + h]
        g_nbr.append(remote(src, dst, g_send.at[0, h], g_recv.at[0, h], z, nbr))
        g_sib.append(remote(src, dst, g_send.at[1, h], g_recv.at[1, h], z, sib))
        held = g_buf.at[nbr * col_blocks + h]
        g_fwd.append(remote(held, held, g_send.at[2, h], g_recv.at[2, h], z, sib))
    for d in range(1, nz):
        panel_copies.append(
            remote(panels_ref.at[c], p_buf.at[z], p_send.at[d - 1], p_recv.at[d - 1], zat(d), c)
        )
    for copy in g_nbr + panel_copies + g_sib:
        copy.start()
    for h in range(col_blocks):
        g_nbr[h].wait_recv()
        g_fwd[h].start()
    for copy in panel_copies + g_sib + g_fwd:
        copy.wait_recv()
    for copy in own_copies + [struct_copy]:
        copy.wait()

    for at in range(0, rows, keep):
        acc = jnp.zeros((keep, width), jnp.float32)
        for p in range(struct_count):
            acc += jnp.dot(
                g_buf[struct_ref[c, p], pl.ds(at, keep), :], p_buf[p],
                preferred_element_type=jnp.float32,
            )
        prod[at:at + keep, :] = acc
        neg[at:at + keep, :] = -acc

    own_cols = pl.ds(pl.multiple_of(c * width, width), width)
    off_copies = []
    for at, ct in enumerate((nbr, dia, sib)):
        off_copies.append(
            remote(neg.at[pl.ds(ct * keep, keep)], off_ref.at[:, own_cols], o_send.at[at], o_recv.at[at], z, ct)
        )

    total = jnp.zeros((width, width), jnp.float32)
    for b in range(row_blocks):
        target = z * row_blocks + b
        place, named = jnp.int32(0), jnp.int32(0)
        for p in range(struct_count):
            hit = struct_ref[c, p] == target
            place = jnp.where(hit, p, place)
            named = jnp.where(hit, 1, named)
        right = prod[b * width:(b + 1) * width, :]
        high = right.astype(jnp.bfloat16)
        low = (right - high.astype(jnp.float32)).astype(jnp.bfloat16)
        left = p_buf[place]
        contract = (((0,), (0,)), ((), ()))
        term = lax.dot_general(left, high, contract, preferred_element_type=jnp.float32)
        term += lax.dot_general(left, low, contract, preferred_element_type=jnp.float32)
        total += term * named.astype(jnp.float32)
    part[...] = total

    sum_copies = []
    for d in range(1, nz):
        sum_copies.append(
            remote(part.at[pl.ds(zat(d) * piece, piece)], rs_buf.at[d - 1], r_send.at[d - 1], r_recv.at[d - 1], zat(d), c)
        )
    for copy in sum_copies + off_copies:
        copy.start()
    off_ref[:, own_cols] = neg[pl.ds(c * keep, keep), :]

    dinv_copy.wait()
    final = dinv_buf[...] + part[pl.ds(z * piece, piece), :]
    for d in range(1, nz):
        sum_copies[d - 1].wait_recv()
        final += rs_buf[d - 1]
    coded = piece % TILE == 0

    def at_piece(ct, j):
        return code.at[ct, j] if coded else diag_ref.at[ct, pl.ds(j * piece, piece)]

    def decode(ct, j):
        if coded:
            power = code[ct, j, piece:, :].astype(jnp.float32)[:1, :]
            step = jnp.exp2(power) * (1.0 / LEVELS)
            diag_ref[ct, pl.ds(j * piece, piece), :] = code[ct, j, :piece, :].astype(jnp.float32) * step

    if coded:
        largest = jnp.max(jnp.abs(final), axis=0, keepdims=True)
        power = jnp.ceil(jnp.log2(jnp.maximum(largest, 1e-30)))
        whole = jnp.round(final * (jnp.exp2(-power) * LEVELS)).astype(jnp.int32)
        code[c, z, :piece, :] = whole.astype(jnp.int16)
        below = jnp.broadcast_to(power, (TILE, width)).astype(jnp.int32)
        code[c, z, piece:, :] = below.astype(jnp.int16)
    else:
        diag_ref[c, pl.ds(z * piece, piece), :] = final

    placed = []

    def place(n, ct):
        placed.append(pltpu.make_async_copy(diag_ref.at[ct], diag_hbm.at[ct], l_sem.at[4 + col_blocks + n]))
        placed[-1].start()

    over_z, over_x, over_k, over_f = [], [], [], []
    for d in range(nz):
        mine, theirs = at_piece(c, zfrom(d)), at_piece(nbr, zfrom(d))
        if d > 0:
            own = at_piece(c, z)
            over_z.append(remote(own, own, a_send.at[d - 1], a_recv.at[d - 1], zat(d), c))
        over_x.append(remote(mine, mine, h_send.at[0, d], h_recv.at[0, d], z, nbr))
        over_k.append(remote(mine, mine, h_send.at[1, d], h_recv.at[1, d], z, sib))
        over_f.append(remote(theirs, theirs, h_send.at[2, d], h_recv.at[2, d], z, sib))
    for copy in over_z:
        copy.start()
    for d in range(nz):
        if d > 0:
            over_z[d - 1].wait_recv()
        over_x[d].start()
        over_k[d].start()
        decode(c, zfrom(d))
    place(0, c)
    for d in range(nz):
        over_x[d].wait_recv()
        over_f[d].start()
        decode(nbr, zfrom(d))
    place(1, nbr)
    for copy in off_copies:
        copy.wait_recv()
    off_out = pltpu.make_async_copy(off_ref, off_hbm, l_sem.at[3 + col_blocks])
    off_out.start()
    for n, copies, ct in ((2, over_k, sib), (3, over_f, dia)):
        for d in range(nz):
            copies[d].wait_recv()
            decode(ct, zfrom(d))
        place(n, ct)
    for copy in g_nbr + g_sib + g_fwd + panel_copies + off_copies + sum_copies + over_z + over_x + over_k + over_f:
        copy.wait_send()
    off_out.wait()
    for copy in placed:
        copy.wait()


def place_kernel(off_ref, diag_ref, off_out, diag_out, off_buf, diag_buf, sem):
    step = off_ref.shape[0] // 2
    parts = [(off_ref, off_out, off_buf, pl.ds(at * step, step)) for at in range(2)]
    parts += [(diag_ref, diag_out, diag_buf, at) for at in range(diag_ref.shape[0])]
    loads, stores = [], []
    for n, (src, dst, buf, part) in enumerate(parts):
        loads.append(pltpu.make_async_copy(src.at[part], buf.at[part], sem.at[0, n]))
        stores.append(pltpu.make_async_copy(buf.at[part], dst.at[part], sem.at[1, n]))
    for copy in loads:
        copy.start()
    for load, store in zip(loads, stores):
        load.wait()
        store.start()
    for copy in stores:
        copy.wait()


def per_device(ginv, panels, structure, dinv):
    super_count, _, width = panels.shape
    nz, nc = lax.axis_size("prow"), lax.axis_size("pcol")
    rows, cols = ginv.shape
    struct_count = structure.shape[1]
    col_blocks = cols // width
    piece = width // nz
    hbm = pl.BlockSpec(memory_space=pl.ANY)
    dma = pltpu.SemaphoreType.DMA
    out_shape = (
        jax.ShapeDtypeStruct((rows // nc, super_count * width), jnp.float32),
        jax.ShapeDtypeStruct((super_count, width, width), jnp.float32),
    )
    off, diag = pl.pallas_call(
        functools.partial(invert_kernel, nz),
        out_shape=out_shape,
        in_specs=[hbm, hbm, hbm, hbm],
        out_specs=(hbm, hbm),
        scratch_shapes=[
            pltpu.SMEM((super_count, struct_count), jnp.int32),
            pltpu.VMEM((nc * col_blocks, rows, width), jnp.bfloat16),
            pltpu.VMEM((struct_count, width, width), jnp.bfloat16),
            pltpu.VMEM((rows, width), jnp.float32),
            pltpu.VMEM((rows, width), jnp.float32),
            pltpu.VMEM((width, width), jnp.float32),
            pltpu.VMEM((nz - 1, piece, width), jnp.float32),
            pltpu.VMEM((piece, width), jnp.float32),
            pltpu.VMEM((rows // nc, super_count * width), jnp.float32),
            pltpu.VMEM((super_count, width, width), jnp.float32),
            pltpu.VMEM((super_count, nz, piece + TILE, width), jnp.int16)
            if piece % TILE == 0 else pltpu.VMEM((8, 128), jnp.float32),
            dma((nz - 1,)), dma((nz - 1,)),
            dma((3, col_blocks)), dma((3, col_blocks)),
            dma((3,)), dma((3,)),
            dma((nz - 1,)), dma((nz - 1,)),
            dma((nz - 1,)), dma((nz - 1,)),
            dma((3, nz)), dma((3, nz)),
            dma((8 + col_blocks,)),
        ],
        compiler_params=pltpu.CompilerParams(
            collective_id=0, has_side_effects=True, vmem_limit_bytes=VMEM_BYTES
        ),
        name="selected_inverse",
    )(ginv, panels, structure, dinv)
    return pl.pallas_call(
        place_kernel,
        out_shape=out_shape,
        in_specs=[hbm, hbm],
        out_specs=(hbm, hbm),
        scratch_shapes=[
            pltpu.VMEM((rows // nc, super_count * width), jnp.float32),
            pltpu.VMEM((super_count, width, width), jnp.float32),
            dma((2, 2 + super_count)),
        ],
        compiler_params=pltpu.CompilerParams(vmem_limit_bytes=VMEM_BYTES),
        name="place_outputs",
    )(off, diag)


def solution(mesh):
    return jax.shard_map(
        per_device,
        mesh=mesh,
        in_specs=(P(("pole", "prow"), "pcol"), P("pole", "prow", None), P(), P("pole", None, None)),
        out_specs=(P(("pole", "prow", "pcol"), None), P("pole", None, None)),
        check_vma=False,
    )
```
